512 devices in a mesh: rep: 32 (over z_hi, y, core), slab: 16 (over z_lo, x).
Axes of the slice: x: 4, y: 8, z: 8 (z_hi: 2, z_lo: 4; z = z_hi * 4 + z_lo), core: 2. Of those that a mesh axis runs over, the one named last changes fastest.
Arguments:
- phi_field: float32 [32, 64, 256, 256], P('rep', 'slab'), may hold values from -4 to 4
- copy_counts: int32 [32], replicated, may hold values from 0 to 4, as said below
- langevin_noise: float32 [2, 32, 64, 256, 256], P(None, 'rep', 'slab'), may hold values from -6 to 6
Outputs:
- new_field: float32 [32, 64, 256, 256], P('rep', 'slab')
The draws below stay inside these ranges and needn't reach their ends.
Inputs may be any that keep to these rules, and one draw needn't show every extreme that they name: copy_counts sum to 32; at least one replica has exactly 4 copies, none has more than 4, and some have none.
All inputs are finite; a program needn't handle non-finite values.
Results may differ from the reference program's by a relative error of at most 0.00002.
Values sent between devices are 32-bit elements; how exact they have to be, the bound alone decides.
No kernel may reach another device: no remote copies, remote signals or barrier semaphores. Data moves between devices by JAX's collectives and lax.ppermute only.
A program may use at most 64 MiB of HBM per device.

```python
import jax
import jax.numpy as jnp
from jax import lax

NY = 256
NX = 256
SWEEPS = 2
NZ = 64
REPLICAS = 32


def draw_copy_counts(key, part):
    key = jax.random.fold_in(key, 7)
    perm_key = jax.random.fold_in(key, 1)
    off_key = jax.random.fold_in(key, 2)
    order = jax.random.permutation(perm_key, REPLICAS).astype(jnp.int32)
    slot_ids = jnp.arange(REPLICAS, dtype=jnp.int32)
    offsets = jax.random.randint(off_key, (REPLICAS,), 0, 4).astype(jnp.int32)
    offsets = jnp.where(slot_ids < 4, 3 - slot_ids, offsets)
    offsets = jnp.minimum(offsets, REPLICAS - 1 - slot_ids)
    picks = order[slot_ids + offsets]
    replica_ids = jnp.arange(REPLICAS, dtype=jnp.int32)
    return jnp.sum((picks[:, None] == replica_ids[None, :]).astype(jnp.int32), axis=0).astype(jnp.int32)


def block_levels(rng, extent, pieces, least, top_value):
    loudness, own = 1.0, jax.random.fold_in(rng, 6)
    for position, blocks in pieces:
        heights = jnp.exp(jax.random.uniform(jax.random.fold_in(own, position), (blocks,), jnp.float32, least / len(pieces), top_value / len(pieces)))
        loudness = loudness * jnp.repeat(heights, extent[position] // blocks).reshape([-1 if axis == position else 1 for axis in range(len(extent))])
    return loudness


def scatter_about(stream_key, dims, deviation, reach, shards=(), held_as=jnp.bfloat16):
    level = block_levels(stream_key, dims, shards, -0.22, 0.18) if shards else 1.0
    result = jax.random.normal(stream_key, dims, jnp.float32) * deviation * level
    return jnp.minimum(jnp.maximum(result, -reach), reach).astype(held_as)


def setup_inputs(seed: int = 0) -> dict:
    keys = jax.random.split(jax.random.key(seed), 4)
    phi_field = scatter_about(keys[0], (REPLICAS, NZ, NY, NX), 1.0, 4.0, ((0, 32), (1, 16)), jnp.float32)
    copy_counts = draw_copy_counts(jax.random.fold_in(keys[3], 71), 0)
    langevin_noise = scatter_about(keys[2], (SWEEPS, REPLICAS, NZ, NY, NX), 1.0, 6.0, ((1, 32), (2, 16)), jnp.float32)
    return dict(phi_field=phi_field, copy_counts=copy_counts, langevin_noise=langevin_noise)


STEP_SIZE = 0.05
MASS_TERM = -0.5
COUPLING = 0.5

def resample_map(copy_counts):
    replica_ids = jnp.arange(copy_counts.shape[0], dtype=jnp.int32)
    extra_copies = jnp.maximum(copy_counts - 1, 0)
    inclusive = jnp.cumsum(extra_copies).astype(jnp.int32)
    empty_slot = (copy_counts == 0).astype(jnp.int32)
    gap_rank = (jnp.cumsum(empty_slot) - empty_slot).astype(jnp.int32)
    filled = lax.optimization_barrier(jnp.sum((inclusive[None, :] <= gap_rank[:, None]).astype(jnp.int32), axis=1)).astype(jnp.int32)
    return jnp.where(copy_counts >= 1, replica_ids, filled).astype(jnp.int32)

def advance(center, neighbor_sum, kicks):
    laplace = neighbor_sum - 6.0 * center
    drift = laplace - MASS_TERM * center - COUPLING * center * center * center
    return center + STEP_SIZE * drift + jnp.sqrt(2.0 * STEP_SIZE) * kicks

def reference(phi_field, copy_counts, langevin_noise):
    source_map = resample_map(copy_counts)
    current = jnp.take(phi_field, source_map, axis=0)
    for sweep_index in range(SWEEPS):
        neighbor_sum = jnp.roll(current, -1, 1) + jnp.roll(current, 1, 1)
        neighbor_sum = neighbor_sum + jnp.roll(current, -1, 2) + jnp.roll(current, 1, 2)
        neighbor_sum = neighbor_sum + jnp.roll(current, -1, 3) + jnp.roll(current, 1, 3)
        current = advance(current, neighbor_sum, langevin_noise[sweep_index])
    return current
```

```python
import functools

import jax
import jax.numpy as jnp
from jax import lax
from jax.experimental import pallas as pl
from jax.experimental.pallas import tpu as pltpu
from jax.sharding import PartitionSpec as P

STEP_SIZE = 0.05
MASS_TERM = -0.5
COUPLING = 0.5
KICK = (2.0 * STEP_SIZE) ** 0.5
HALF = 16
STRIP = 32
VMEM = pl.BlockSpec(memory_space=pltpu.VMEM)
SMEM = pl.BlockSpec(memory_space=pltpu.SMEM)
PARAMS = pltpu.CompilerParams(vmem_limit_bytes=10 * 1024 * 1024)


def cost(flops, size):
    return pl.CostEstimate(flops=flops, bytes_accessed=size, transcendentals=0)


def ring_order():
    return [((3 * y) % 8) * 2 + core for y in range(8) for core in range(2)]


def exchange(parts, order):
    groups = [[half * HALF + i for i in order] for half in range(2)]
    return lax.all_to_all(parts, "rep", split_axis=0, concat_axis=0, tiled=True, axis_index_groups=groups)


def resample_map(copy_counts):
    ids = jnp.arange(copy_counts.shape[0], dtype=jnp.int32)
    upto = ids[None, :] <= ids[:, None]
    extra = jnp.maximum(copy_counts - 1, 0)
    inclusive = jnp.sum(jnp.where(upto, extra[None, :], 0), axis=1)
    empty = (copy_counts == 0).astype(jnp.int32)
    rank = jnp.sum(jnp.where(upto, empty[None, :], 0), axis=1) - empty
    filled = jnp.sum((inclusive[None, :] <= rank[:, None]).astype(jnp.int32), axis=1)
    return jnp.where(copy_counts >= 1, ids, filled)


def routes(copy_counts, order):
    ids = jnp.arange(2 * HALF, dtype=jnp.int32)
    half = lax.axis_index("rep") // HALF
    place = jnp.array([order.index(i) for i in range(HALF)] * 2, jnp.int32)
    source_map = resample_map(copy_counts)
    crosses = source_map // HALF != ids // HALF
    asked = source_map[:, None] == ids[None, :]
    wanted = jnp.any(crosses[:, None] & asked, axis=0)
    count = jnp.sum(wanted.astype(jnp.int32))
    earlier = (ids[None, :] < ids[:, None]) & wanted[None, :]
    rank = jnp.sum(earlier.astype(jnp.int32), axis=1)
    mine = wanted & (ids // HALF == half)
    send = jnp.sum(jnp.where(mine[None, :] & (rank[None, :] == ids[:HALF, None]), place[None, :], 0), axis=1)
    target = jnp.array(order, jnp.int32) + half * HALF
    where_from = jnp.where(ids // HALF == half, place, HALF + rank)
    source = jnp.sum(jnp.where(target[:, None] == ids[None, :], source_map[None, :], 0), axis=1)
    pick = jnp.sum(jnp.where(source[:, None] == ids[None, :], where_from[None, :], 0), axis=1)
    return pick, send, count


def chosen_parts(spread, pick, send, count):
    swap = [(i, (i + HALF) % (2 * HALF)) for i in range(2 * HALF)]

    def crossing(width, spread, pick, send):
        if width == 0:
            return jnp.take(spread, pick, axis=0, mode="clip")
        far = lax.ppermute(jnp.take(spread, send[:width], axis=0, mode="clip"), "rep", swap)
        return jnp.take(jnp.concatenate([spread, far]), pick, axis=0, mode="clip")

    widths = (0, 1, 2, 4, HALF)
    case = sum((count > w).astype(jnp.int32) for w in widths[:-1])
    return lax.switch(case, [functools.partial(crossing, w) for w in widths], spread, pick, send)


def step(ref, plane, start, along_z, kicks):
    rows = lambda first, size: ref[plane, pl.ds(pl.multiple_of(first, 8), size), :]
    center = rows(start, STRIP)
    block = jnp.concatenate([rows((start + 248) % 256, 8), center, rows((start + STRIP) % 256, 8)])
    above = pltpu.roll(block, STRIP + 15, 0)[8 : 8 + STRIP]
    below = pltpu.roll(block, 1, 0)[8 : 8 + STRIP]
    right, left = pltpu.roll(center, 255, 1), pltpu.roll(center, 1, 1)
    laplace = along_z + above + below + right + left - 6.0 * center
    drift = laplace - MASS_TERM * center - COUPLING * center * center * center
    return center + STEP_SIZE * drift + kicks


def strips(body):
    @pl.loop(0, 256 // STRIP)
    def _(i):
        start = pl.multiple_of(i * STRIP, STRIP)
        body(start, pl.ds(start, STRIP))


def edge_kernel(even, field, noise, edge, inner, outer):
    def body(start, here):
        edge[0, here, :] = step(field, 0, start, field[1, here, :], KICK * noise[0, 0, here, :])
        edge[1, here, :] = step(field, 3, start, field[2, here, :], KICK * noise[0, 3, here, :])

    strips(body)

    def fill(below, above):
        below[0] = field[0]
        below[1] = edge[0]
        above[0] = field[3]
        above[1] = edge[1]

    @pl.when(even[0] == 1)
    def _():
        fill(outer, inner)

    @pl.when(even[0] == 0)
    def _():
        fill(inner, outer)


def late_kernel(even, field, edge, first, second, middle, later, last, out, sides):
    def near(below, above):
        def body(start, here):
            sides[0, here, :] = below[1, here, :] + STEP_SIZE * field[0, here, :] + middle[0, here, :]
            sides[3, here, :] = above[1, here, :] + STEP_SIZE * field[3, here, :] + middle[1, here, :]
            low = edge[0, here, :] + STEP_SIZE * below[0, here, :]
            high = edge[1, here, :] + STEP_SIZE * above[0, here, :]
            sides[1, here, :] = low
            sides[2, here, :] = high
            out[1, here, :] = later[0, here, :] + STEP_SIZE * low
            out[2, here, :] = later[1, here, :] + STEP_SIZE * high

        strips(body)

    @pl.when(even[0] == 1)
    def _():
        near(second, first)

    @pl.when(even[0] == 0)
    def _():
        near(first, second)

    def end(start, here):
        out[0, here, :] = step(sides, 1, start, sides[0, here, :], last[0, here, :])
        out[3, here, :] = step(sides, 2, start, sides[3, here, :], last[1, here, :])

    strips(end)


def swept(center, along_z, kicks):
    total = along_z + jnp.roll(center, -1, 1) + jnp.roll(center, 1, 1)
    total = total + jnp.roll(center, -1, 2) + jnp.roll(center, 1, 2)
    laplace = total - 6.0 * center
    drift = laplace - MASS_TERM * center - COUPLING * center * center * center
    return center + STEP_SIZE * drift + KICK * kicks


def shards(phi_field, copy_counts, langevin_noise):
    planes, height, width = phi_field.shape[1:]
    size = lax.axis_size("slab")
    order = ring_order()
    noise = langevin_noise[:, 0]
    spread = exchange(phi_field.reshape(HALF, -1, width), order)
    route = routes(copy_counts, order)
    field = exchange(chosen_parts(spread, *route), order).reshape(planes, height, width)
    even = (lax.axis_index("slab") % 2 == 0).astype(jnp.int32).reshape(1)
    pair = jax.ShapeDtypeStruct((2, height, width), jnp.float32)
    plane = 4 * height * width
    edge, inner, outer = pl.pallas_call(
        edge_kernel,
        out_shape=[pair] * 3,
        in_specs=[SMEM] + [VMEM] * 2,
        out_specs=[VMEM] * 3,
        compiler_params=PARAMS,
        cost_estimate=cost(2 * 16 * plane // 4, 12 * plane),
    )(even, field, noise)
    inner, outer, field = lax.optimization_barrier((inner, outer, field))
    first = lax.ppermute(inner, "slab", [(i, i ^ 1) for i in range(size)])
    second = lax.ppermute(outer, "slab", [(i, (i - 1 + 2 * (i % 2)) % size) for i in range(size)])
    middle = swept(field[1:3], field[2:4] + field[0:2], noise[0, 1:3])
    later = swept(middle, middle[::-1], noise[1, 1:3])
    last = KICK * jnp.concatenate([noise[1, :1], noise[1, 3:]])
    out = pl.pallas_call(
        late_kernel,
        out_shape=jax.ShapeDtypeStruct((planes, height, width), jnp.float32),
        in_specs=[SMEM] + [VMEM] * 7,
        out_specs=VMEM,
        scratch_shapes=[pltpu.VMEM((4, height, width), jnp.float32)],
        compiler_params=PARAMS,
        cost_estimate=cost(3 * 16 * plane // 4, 20 * plane),
    )(even, field, edge, first, second, middle, later, last)
    return out[None]


def solution(mesh):
    return jax.shard_map(
        shards,
        mesh=mesh,
        in_specs=(P("rep", "slab", None, None), P(), P(None, "rep", "slab", None, None)),
        out_specs=P("rep", "slab", None, None),
        check_vma=False,
    )
```

```python
import functools

import jax
import jax.numpy as jnp
from jax import lax
from jax.experimental import pallas as pl
from jax.experimental.pallas import tpu as pltpu
from jax.sharding import PartitionSpec as P

STEP_SIZE = 0.05
MASS_TERM = -0.5
COUPLING = 0.5
KICK = (2.0 * STEP_SIZE) ** 0.5
HALF = 16
STRIP = 32
VMEM = pl.BlockSpec(memory_space=pltpu.VMEM)
SMEM = pl.BlockSpec(memory_space=pltpu.SMEM)
PARAMS = pltpu.CompilerParams(vmem_limit_bytes=10 * 1024 * 1024)


def cost(flops, size):
    return pl.CostEstimate(flops=flops, bytes_accessed=size, transcendentals=0)


def ring_order():
    return [((3 * y) % 8) * 2 + core for y in range(8) for core in range(2)]


def exchange(parts, order):
    groups = [[half * HALF + i for i in order] for half in range(2)]
    return lax.all_to_all(parts, "rep", split_axis=0, concat_axis=0, tiled=True, axis_index_groups=groups)


def resample_map(copy_counts):
    ids = jnp.arange(copy_counts.shape[0], dtype=jnp.int32)
    upto = ids[None, :] <= ids[:, None]
    extra = jnp.maximum(copy_counts - 1, 0)
    inclusive = jnp.sum(jnp.where(upto, extra[None, :], 0), axis=1)
    empty = (copy_counts == 0).astype(jnp.int32)
    rank = jnp.sum(jnp.where(upto, empty[None, :], 0), axis=1) - empty
    filled = jnp.sum((inclusive[None, :] <= rank[:, None]).astype(jnp.int32), axis=1)
    return jnp.where(copy_counts >= 1, ids, filled)


def routes(copy_counts, order):
    ids = jnp.arange(2 * HALF, dtype=jnp.int32)
    half = lax.axis_index("rep") // HALF
    place = jnp.array([order.index(i) for i in range(HALF)] * 2, jnp.int32)
    source_map = resample_map(copy_counts)
    crosses = source_map // HALF != ids // HALF
    asked = source_map[:, None] == ids[None, :]
    wanted = jnp.any(crosses[:, None] & asked, axis=0)
    count = jnp.sum(wanted.astype(jnp.int32))
    earlier = (ids[None, :] < ids[:, None]) & wanted[None, :]
    rank = jnp.sum(earlier.astype(jnp.int32), axis=1)
    mine = wanted & (ids // HALF == half)
    send = jnp.sum(jnp.where(mine[None, :] & (rank[None, :] == ids[:HALF, None]), place[None, :], 0), axis=1)
    target = jnp.array(order, jnp.int32) + half * HALF
    where_from = jnp.where(ids // HALF == half, place, HALF + rank)
    source = jnp.sum(jnp.where(target[:, None] == ids[None, :], source_map[None, :], 0), axis=1)
    pick = jnp.sum(jnp.where(source[:, None] == ids[None, :], where_from[None, :], 0), axis=1)
    return pick, send, count


def chosen_parts(spread, pick, send, count):
    swap = [(i, (i + HALF) % (2 * HALF)) for i in range(2 * HALF)]

    def crossing(width, spread, pick, send):
        if width == HALF:
            far = lax.ppermute(jnp.take(spread, send, axis=0, mode="clip"), "rep", swap)
            return jnp.take(jnp.concatenate([spread, far]), pick, axis=0, mode="clip")
        if width:
            far = lax.ppermute(jnp.take(spread, send[:width], axis=0, mode="clip"), "rep", swap)
        parts = jnp.take(spread, pick, axis=0, mode="clip")
        for i in range(width):
            parts = jnp.where((pick == HALF + i)[:, None, None], far[i : i + 1], parts)
        return parts

    widths = (0, 1, 2, 4, HALF)
    case = sum((count > w).astype(jnp.int32) for w in widths[:-1])
    return lax.switch(case, [functools.partial(crossing, w) for w in widths], spread, pick, send)


def step(ref, plane, start, along_z, kicks):
    rows = lambda first, size: ref[plane, pl.ds(pl.multiple_of(first, 8), size), :]
    center = rows(start, STRIP)
    block = jnp.concatenate([rows((start + 248) % 256, 8), center, rows((start + STRIP) % 256, 8)])
    above = pltpu.roll(block, STRIP + 15, 0)[8 : 8 + STRIP]
    below = pltpu.roll(block, 1, 0)[8 : 8 + STRIP]
    right, left = pltpu.roll(center, 255, 1), pltpu.roll(center, 1, 1)
    laplace = along_z + above + below + right + left - 6.0 * center
    drift = laplace - MASS_TERM * center - COUPLING * center * center * center
    return center + STEP_SIZE * drift + kicks


def strips(body):
    @pl.loop(0, 256 // STRIP)
    def _(i):
        start = pl.multiple_of(i * STRIP, STRIP)
        body(start, pl.ds(start, STRIP))


def edge_kernel(even, field, noise, edge, middle, inner, outer):
    def body(start, here):
        edge[0, here, :] = step(field, 0, start, field[1, here, :], KICK * noise[0, 0, here, :])
        edge[1, here, :] = step(field, 3, start, field[2, here, :], KICK * noise[0, 3, here, :])
        for plane in (1, 2):
            along_z = field[plane + 1, here, :] + field[plane - 1, here, :]
            middle[plane - 1, here, :] = step(field, plane, start, along_z, KICK * noise[0, plane, here, :])

    strips(body)

    def fill(below, above):
        below[0] = field[0]
        below[1] = edge[0]
        above[0] = field[3]
        above[1] = edge[1]

    @pl.when(even[0] == 1)
    def _():
        fill(outer, inner)

    @pl.when(even[0] == 0)
    def _():
        fill(inner, outer)


def late_kernel(even, field, edge, first, second, middle, later, last, out, sides):
    def near(below, above):
        def body(start, here):
            sides[0, here, :] = below[1, here, :] + STEP_SIZE * field[0, here, :] + middle[0, here, :]
            sides[3, here, :] = above[1, here, :] + STEP_SIZE * field[3, here, :] + middle[1, here, :]
            low = edge[0, here, :] + STEP_SIZE * below[0, here, :]
            high = edge[1, here, :] + STEP_SIZE * above[0, here, :]
            sides[1, here, :] = low
            sides[2, here, :] = high
            out[1, here, :] = later[0, here, :] + STEP_SIZE * low
            out[2, here, :] = later[1, here, :] + STEP_SIZE * high

        strips(body)

    @pl.when(even[0] == 1)
    def _():
        near(second, first)

    @pl.when(even[0] == 0)
    def _():
        near(first, second)

    def end(start, here):
        out[0, here, :] = step(sides, 1, start, sides[0, here, :], last[0, here, :])
        out[3, here, :] = step(sides, 2, start, sides[3, here, :], last[1, here, :])

    strips(end)


def side_swap(turn, size):
    pairs = []
    for rep in range(2 * HALF):
        for slab in range(size):
            above = (slab + rep + turn) % 2 == 0
            pairs.append((rep * size + slab, rep * size + (slab + (1 if above else -1)) % size))
    return pairs


def swept(center, along_z, kicks):
    total = along_z + jnp.roll(center, -1, 1) + jnp.roll(center, 1, 1)
    total = total + jnp.roll(center, -1, 2) + jnp.roll(center, 1, 2)
    laplace = total - 6.0 * center
    drift = laplace - MASS_TERM * center - COUPLING * center * center * center
    return center + STEP_SIZE * drift + KICK * kicks


def shards(phi_field, copy_counts, langevin_noise):
    planes, height, width = phi_field.shape[1:]
    size = lax.axis_size("slab")
    order = ring_order()
    noise = langevin_noise[:, 0]
    spread = exchange(phi_field.reshape(HALF, -1, width), order)
    route = routes(copy_counts, order)
    field = exchange(chosen_parts(spread, *route), order).reshape(planes, height, width)
    even = ((lax.axis_index("slab") + lax.axis_index("rep")) % 2 == 0).astype(jnp.int32).reshape(1)
    pair = jax.ShapeDtypeStruct((2, height, width), jnp.float32)
    plane = 4 * height * width
    edge, middle, inner, outer = pl.pallas_call(
        edge_kernel,
        out_shape=[pair] * 4,
        in_specs=[SMEM] + [VMEM] * 2,
        out_specs=[VMEM] * 4,
        compiler_params=PARAMS,
        cost_estimate=cost(2 * 16 * plane // 4, 12 * plane),
    )(even, field, noise)
    first = lax.ppermute(inner, ("rep", "slab"), side_swap(0, size))
    second = lax.ppermute(outer, ("rep", "slab"), side_swap(1, size))
    later = swept(middle, middle[::-1], noise[1, 1:3])
    last = KICK * jnp.concatenate([noise[1, :1], noise[1, 3:]])
    out = pl.pallas_call(
        late_kernel,
        out_shape=jax.ShapeDtypeStruct((planes, height, width), jnp.float32),
        in_specs=[SMEM] + [VMEM] * 7,
        out_specs=VMEM,
        scratch_shapes=[pltpu.VMEM((4, height, width), jnp.float32)],
        compiler_params=PARAMS,
        cost_estimate=cost(3 * 16 * plane // 4, 20 * plane),
    )(even, field, edge, first, second, middle, later, last)
    return out[None]


def solution(mesh):
    return jax.shard_map(
        shards,
        mesh=mesh,
        in_specs=(P("rep", "slab", None, None), P(), P(None, "rep", "slab", None, None)),
        out_specs=P("rep", "slab", None, None),
        check_vma=False,
    )
```

```python
import functools

import jax
import jax.numpy as jnp
from jax import lax
from jax.experimental import pallas as pl
from jax.experimental.pallas import tpu as pltpu
from jax.sharding import PartitionSpec as P

STEP_SIZE = 0.05
MASS_TERM = -0.5
COUPLING = 0.5
KICK = (2.0 * STEP_SIZE) ** 0.5
HALF = 16
STRIP = 32
VMEM = pl.BlockSpec(memory_space=pltpu.VMEM)
SMEM = pl.BlockSpec(memory_space=pltpu.SMEM)
PARAMS = pltpu.CompilerParams(vmem_limit_bytes=10 * 1024 * 1024)


def cost(flops, size):
    return pl.CostEstimate(flops=flops, bytes_accessed=size, transcendentals=0)


def ring_order():
    return [((3 * y) % 8) * 2 + core for y in range(8) for core in range(2)]


def exchange(parts, order):
    groups = [[half * HALF + i for i in order] for half in range(2)]
    return lax.all_to_all(parts, "rep", split_axis=0, concat_axis=0, tiled=True, axis_index_groups=groups)


def resample_map(copy_counts):
    ids = jnp.arange(copy_counts.shape[0], dtype=jnp.int32)
    upto = ids[None, :] <= ids[:, None]
    extra = jnp.maximum(copy_counts - 1, 0)
    inclusive = jnp.sum(jnp.where(upto, extra[None, :], 0), axis=1)
    empty = (copy_counts == 0).astype(jnp.int32)
    rank = jnp.sum(jnp.where(upto, empty[None, :], 0), axis=1) - empty
    filled = jnp.sum((inclusive[None, :] <= rank[:, None]).astype(jnp.int32), axis=1)
    return jnp.where(copy_counts >= 1, ids, filled)


def routes(copy_counts, order):
    ids = jnp.arange(2 * HALF, dtype=jnp.int32)
    half = lax.axis_index("rep") // HALF
    place = jnp.array([order.index(i) for i in range(HALF)] * 2, jnp.int32)
    source_map = resample_map(copy_counts)
    crosses = source_map // HALF != ids // HALF
    asked = source_map[:, None] == ids[None, :]
    wanted = jnp.any(crosses[:, None] & asked, axis=0)
    count = jnp.sum(wanted.astype(jnp.int32))
    earlier = (ids[None, :] < ids[:, None]) & wanted[None, :]
    rank = jnp.sum(earlier.astype(jnp.int32), axis=1)
    mine = wanted & (ids // HALF == half)
    send = jnp.sum(jnp.where(mine[None, :] & (rank[None, :] == ids[:HALF, None]), place[None, :], 0), axis=1)
    target = jnp.array(order, jnp.int32) + half * HALF
    where_from = jnp.where(ids // HALF == half, place, HALF + rank)
    source = jnp.sum(jnp.where(target[:, None] == ids[None, :], source_map[None, :], 0), axis=1)
    pick = jnp.sum(jnp.where(source[:, None] == ids[None, :], where_from[None, :], 0), axis=1)
    return pick, send, count, jnp.any(wanted[:HALF])


def chosen_parts(spread, pick, send, count, upward):
    def kept(spread, pick, send):
        return jnp.take(spread, pick, axis=0, mode="clip")

    def crossing(width, source, spread, pick, send):
        pairs = [(source * HALF + i, (1 - source) * HALF + i) for i in range(HALF)]
        far = lax.ppermute(jnp.take(spread, send[:width], axis=0, mode="clip"), "rep", pairs)
        if width == HALF:
            return jnp.take(jnp.concatenate([spread, far]), pick, axis=0, mode="clip")
        parts = kept(spread, pick, send)
        for i in range(width):
            parts = jnp.where((pick == HALF + i)[:, None, None], far[i : i + 1], parts)
        return parts

    widths = (1, 2, 3, 4, 6, HALF)
    case = sum((count > w).astype(jnp.int32) for w in widths[:-1])
    case = jnp.where(count == 0, 0, 1 + case + jnp.where(upward, 0, len(widths)))
    branches = [kept] + [functools.partial(crossing, w, source) for source in range(2) for w in widths]
    return lax.switch(case, branches, spread, pick, send)


def step(ref, plane, start, along_z, kicks):
    rows = lambda first, size: ref[plane, pl.ds(pl.multiple_of(first, 8), size), :]
    center = rows(start, STRIP)
    block = jnp.concatenate([rows((start + 248) % 256, 8), center, rows((start + STRIP) % 256, 8)])
    above = pltpu.roll(block, STRIP + 15, 0)[8 : 8 + STRIP]
    below = pltpu.roll(block, 1, 0)[8 : 8 + STRIP]
    right, left = pltpu.roll(center, 255, 1), pltpu.roll(center, 1, 1)
    laplace = along_z + above + below + right + left - 6.0 * center
    drift = laplace - MASS_TERM * center - COUPLING * center * center * center
    return center + STEP_SIZE * drift + kicks


def strips(body):
    @pl.loop(0, 256 // STRIP)
    def _(i):
        start = pl.multiple_of(i * STRIP, STRIP)
        body(start, pl.ds(start, STRIP))


def edge_kernel(even, field, noise, edge, middle, inner, outer):
    def body(start, here):
        edge[0, here, :] = step(field, 0, start, field[1, here, :], KICK * noise[0, 0, here, :])
        edge[1, here, :] = step(field, 3, start, field[2, here, :], KICK * noise[0, 3, here, :])
        for plane in (1, 2):
            along_z = field[plane + 1, here, :] + field[plane - 1, here, :]
            middle[plane - 1, here, :] = step(field, plane, start, along_z, KICK * noise[0, plane, here, :])

    strips(body)

    def fill(below, above):
        below[0] = field[0]
        below[1] = edge[0]
        above[0] = field[3]
        above[1] = edge[1]

    @pl.when(even[0] == 1)
    def _():
        fill(outer, inner)

    @pl.when(even[0] == 0)
    def _():
        fill(inner, outer)


def late_kernel(even, field, edge, first, second, middle, later, last, out, sides):
    def near(below, above):
        def body(start, here):
            sides[0, here, :] = below[1, here, :] + STEP_SIZE * field[0, here, :] + middle[0, here, :]
            sides[3, here, :] = above[1, here, :] + STEP_SIZE * field[3, here, :] + middle[1, here, :]
            low = edge[0, here, :] + STEP_SIZE * below[0, here, :]
            high = edge[1, here, :] + STEP_SIZE * above[0, here, :]
            sides[1, here, :] = low
            sides[2, here, :] = high
            out[1, here, :] = later[0, here, :] + STEP_SIZE * low
            out[2, here, :] = later[1, here, :] + STEP_SIZE * high

        strips(body)

    @pl.when(even[0] == 1)
    def _():
        near(second, first)

    @pl.when(even[0] == 0)
    def _():
        near(first, second)

    def end(start, here):
        out[0, here, :] = step(sides, 1, start, sides[0, here, :], last[0, here, :])
        out[3, here, :] = step(sides, 2, start, sides[3, here, :], last[1, here, :])

    strips(end)


def side_swap(turn, size):
    pairs = []
    for rep in range(2 * HALF):
        for slab in range(size):
            above = (slab + rep + turn) % 2 == 0
            pairs.append((rep * size + slab, rep * size + (slab + (1 if above else -1)) % size))
    return pairs


def swept(center, along_z, kicks):
    total = along_z + jnp.roll(center, -1, 1) + jnp.roll(center, 1, 1)
    total = total + jnp.roll(center, -1, 2) + jnp.roll(center, 1, 2)
    laplace = total - 6.0 * center
    drift = laplace - MASS_TERM * center - COUPLING * center * center * center
    return center + STEP_SIZE * drift + KICK * kicks


def shards(phi_field, copy_counts, langevin_noise):
    planes, height, width = phi_field.shape[1:]
    size = lax.axis_size("slab")
    order = ring_order()
    noise = langevin_noise[:, 0]
    spread = exchange(phi_field.reshape(HALF, -1, width), order)
    route = routes(copy_counts, order)
    field = exchange(chosen_parts(spread, *route), order).reshape(planes, height, width)
    even = ((lax.axis_index("slab") + lax.axis_index("rep")) % 2 == 0).astype(jnp.int32).reshape(1)
    pair = jax.ShapeDtypeStruct((2, height, width), jnp.float32)
    plane = 4 * height * width
    edge, middle, inner, outer = pl.pallas_call(
        edge_kernel,
        out_shape=[pair] * 4,
        in_specs=[SMEM] + [VMEM] * 2,
        out_specs=[VMEM] * 4,
        compiler_params=PARAMS,
        cost_estimate=cost(2 * 16 * plane // 4, 12 * plane),
    )(even, field, noise)
    first = lax.ppermute(inner, ("rep", "slab"), side_swap(0, size))
    second = lax.ppermute(outer, ("rep", "slab"), side_swap(1, size))
    later = swept(middle, middle[::-1], noise[1, 1:3])
    last = KICK * jnp.concatenate([noise[1, :1], noise[1, 3:]])
    out = pl.pallas_call(
        late_kernel,
        out_shape=jax.ShapeDtypeStruct((planes, height, width), jnp.float32),
        in_specs=[SMEM] + [VMEM] * 7,
        out_specs=VMEM,
        scratch_shapes=[pltpu.VMEM((4, height, width), jnp.float32)],
        compiler_params=PARAMS,
        cost_estimate=cost(3 * 16 * plane // 4, 20 * plane),
    )(even, field, edge, first, second, middle, later, last)
    return out[None]


def solution(mesh):
    return jax.shard_map(
        shards,
        mesh=mesh,
        in_specs=(P("rep", "slab", None, None), P(), P(None, "rep", "slab", None, None)),
        out_specs=P("rep", "slab", None, None),
        check_vma=False,
    )
```

```python
import functools

import jax
import jax.numpy as jnp
from jax import lax
from jax.experimental import pallas as pl
from jax.experimental.pallas import tpu as pltpu
from jax.sharding import PartitionSpec as P

STEP_SIZE = 0.05
MASS_TERM = -0.5
COUPLING = 0.5
KICK = (2.0 * STEP_SIZE) ** 0.5
HALF = 16
STRIP = 64
VMEM = pl.BlockSpec(memory_space=pltpu.VMEM)
SMEM = pl.BlockSpec(memory_space=pltpu.SMEM)
HBM = pl.BlockSpec(memory_space=pl.ANY)
PARAMS = pltpu.CompilerParams(vmem_limit_bytes=10 * 1024 * 1024)


def cost(flops, size):
    return pl.CostEstimate(flops=flops, bytes_accessed=size, transcendentals=0)


def ring_order():
    return [((3 * y) % 8) * 2 + core for y in range(8) for core in range(2)]


def exchange(parts, order):
    groups = [[half * HALF + i for i in order] for half in range(2)]
    return lax.all_to_all(parts, "rep", split_axis=0, concat_axis=0, tiled=True, axis_index_groups=groups)


def resample_map(copy_counts):
    ids = jnp.arange(copy_counts.shape[0], dtype=jnp.int32)
    upto = ids[None, :] <= ids[:, None]
    extra = jnp.maximum(copy_counts - 1, 0)
    inclusive = jnp.sum(jnp.where(upto, extra[None, :], 0), axis=1)
    empty = (copy_counts == 0).astype(jnp.int32)
    rank = jnp.sum(jnp.where(upto, empty[None, :], 0), axis=1) - empty
    filled = jnp.sum((inclusive[None, :] <= rank[:, None]).astype(jnp.int32), axis=1)
    return jnp.where(copy_counts >= 1, ids, filled)


def routes(copy_counts, order):
    ids = jnp.arange(2 * HALF, dtype=jnp.int32)
    half = lax.axis_index("rep") // HALF
    place = jnp.array([order.index(i) for i in range(HALF)] * 2, jnp.int32)
    source_map = resample_map(copy_counts)
    crosses = source_map // HALF != ids // HALF
    asked = source_map[:, None] == ids[None, :]
    wanted = jnp.any(crosses[:, None] & asked, axis=0)
    count = jnp.sum(wanted.astype(jnp.int32))
    earlier = (ids[None, :] < ids[:, None]) & wanted[None, :]
    rank = jnp.sum(earlier.astype(jnp.int32), axis=1)
    mine = wanted & (ids // HALF == half)
    send = jnp.sum(jnp.where(mine[None, :] & (rank[None, :] == ids[:HALF, None]), place[None, :], 0), axis=1)
    target = jnp.array(order, jnp.int32) + half * HALF
    where_from = jnp.where(ids // HALF == half, place, HALF + rank)
    source = jnp.sum(jnp.where(target[:, None] == ids[None, :], source_map[None, :], 0), axis=1)
    pick = jnp.sum(jnp.where(source[:, None] == ids[None, :], where_from[None, :], 0), axis=1)
    return pick, send, count, jnp.any(wanted[:HALF])


def chosen_parts(spread, pick, send, count, upward):
    def kept(spread, pick, send):
        return jnp.take(spread, pick, axis=0, mode="clip")

    def crossing(width, source, spread, pick, send):
        pairs = [(source * HALF + i, (1 - source) * HALF + i) for i in range(HALF)]
        far = lax.ppermute(jnp.take(spread, send[:width], axis=0, mode="clip"), "rep", pairs)
        if width == HALF:
            return jnp.take(jnp.concatenate([spread, far]), pick, axis=0, mode="clip")
        parts = kept(spread, pick, send)
        for i in range(width):
            parts = jnp.where((pick == HALF + i)[:, None, None], far[i : i + 1], parts)
        return parts

    widths = (1, 2, 3, 4, 6, HALF)
    case = sum((count > w).astype(jnp.int32) for w in widths[:-1])
    case = jnp.where(count == 0, 0, 1 + case + jnp.where(upward, 0, len(widths)))
    branches = [kept] + [functools.partial(crossing, w, source) for source in range(2) for w in widths]
    return lax.switch(case, branches, spread, pick, send)


def step(ref, plane, start, along_z, kicks):
    rows = lambda first, size: ref[plane, pl.ds(pl.multiple_of(first, 8), size), :]
    center = rows(start, STRIP)
    block = jnp.concatenate([rows((start + 248) % 256, 8), center, rows((start + STRIP) % 256, 8)])
    above = pltpu.roll(block, STRIP + 15, 0)[8 : 8 + STRIP]
    below = pltpu.roll(block, 1, 0)[8 : 8 + STRIP]
    right, left = pltpu.roll(center, 255, 1), pltpu.roll(center, 1, 1)
    laplace = along_z + above + below + right + left - 6.0 * center
    drift = laplace - MASS_TERM * center - COUPLING * center * center * center
    return center + STEP_SIZE * drift + kicks


def strips(body):
    @pl.loop(0, 256 // STRIP)
    def _(i):
        start = pl.multiple_of(i * STRIP, STRIP)
        body(start, pl.ds(start, STRIP))


def edge_kernel(even, field, noise, edge, inner, outer):
    def fill(below, above):
        def body(start, here):
            low = step(field, 0, start, field[1, here, :], KICK * noise[0, 0, here, :])
            high = step(field, 3, start, field[2, here, :], KICK * noise[0, 3, here, :])
            edge[0, here, :] = low
            edge[1, here, :] = high
            below[0, here, :] = field[0, here, :]
            below[1, here, :] = low
            above[0, here, :] = field[3, here, :]
            above[1, here, :] = high

        strips(body)

    @pl.when(even[0] == 1)
    def _():
        fill(outer, inner)

    @pl.when(even[0] == 0)
    def _():
        fill(inner, outer)


def near_kernel(even, field, edge, first, noise, rest, out, middle, ends, sems):
    def inside(start, here):
        for plane in (1, 2):
            along_z = field[plane + 1, here, :] + field[plane - 1, here, :]
            middle[plane - 1, here, :] = step(field, plane, start, along_z, KICK * noise[0, plane, here, :])

    def side(end, near, far):
        def completed(start, here):
            swept_end = edge[end // 3, here, :] + STEP_SIZE * first[0, here, :]
            middle[2, here, :] = swept_end
            inner = step(middle, near - 1, start, middle[far - 1, here, :], KICK * noise[1, near, here, :])
            ends[1, here, :] = inner + STEP_SIZE * swept_end
            rest[0, here, :] = middle[far - 1, here, :]
            rest[1, here, :] = step(middle, far - 1, start, middle[near - 1, here, :], KICK * noise[1, far, here, :])

        def last(start, here):
            beyond = first[1, here, :] + STEP_SIZE * field[end, here, :]
            along_z = middle[near - 1, here, :] + beyond
            ends[0, here, :] = step(middle, 2, start, along_z, KICK * noise[1, end, here, :])

        strips(completed)
        inner_copy = pltpu.make_async_copy(ends.at[1], out.at[near], sems.at[1])
        inner_copy.start()
        strips(last)
        end_copy = pltpu.make_async_copy(ends.at[0], out.at[end], sems.at[0])
        end_copy.start()
        inner_copy.wait()
        end_copy.wait()

    strips(inside)

    @pl.when(even[0] == 1)
    def _():
        side(3, 2, 1)

    @pl.when(even[0] == 0)
    def _():
        side(0, 1, 2)


def far_kernel(even, field, edge, second, kicks, rest, started, out, whole, ends, sems):
    def side(end, inner):
        def completed(start, here):
            swept_end = edge[end // 3, here, :] + STEP_SIZE * second[0, here, :]
            whole[0, here, :] = swept_end
            ends[1, here, :] = rest[1, here, :] + STEP_SIZE * swept_end

        def last(start, here):
            beyond = second[1, here, :] + STEP_SIZE * field[end, here, :]
            ends[0, here, :] = step(whole, 0, start, rest[0, here, :] + beyond, KICK * kicks[end // 3, here, :])

        strips(completed)
        inner_copy = pltpu.make_async_copy(ends.at[1], out.at[inner], sems.at[1])
        inner_copy.start()
        strips(last)
        end_copy = pltpu.make_async_copy(ends.at[0], out.at[end], sems.at[0])
        end_copy.start()
        inner_copy.wait()
        end_copy.wait()

    @pl.when(even[0] == 1)
    def _():
        side(0, 1)

    @pl.when(even[0] == 0)
    def _():
        side(3, 2)


def side_swap(turn, size):
    pairs = []
    for rep in range(2 * HALF):
        for slab in range(size):
            above = (slab + rep + turn) % 2 == 0
            pairs.append((rep * size + slab, rep * size + (slab + (1 if above else -1)) % size))
    return pairs


def shards(phi_field, copy_counts, langevin_noise):
    planes, height, width = phi_field.shape[1:]
    size = lax.axis_size("slab")
    order = ring_order()
    noise = langevin_noise[:, 0]
    spread = exchange(phi_field.reshape(HALF, -1, width), order)
    route = routes(copy_counts, order)
    field = exchange(chosen_parts(spread, *route), order).reshape(planes, height, width)
    even = ((lax.axis_index("slab") + lax.axis_index("rep")) % 2 == 0).astype(jnp.int32).reshape(1)
    pair = jax.ShapeDtypeStruct((2, height, width), jnp.float32)
    plane = 4 * height * width
    edge, inner, outer = pl.pallas_call(
        edge_kernel,
        out_shape=[pair] * 3,
        in_specs=[SMEM] + [VMEM] * 2,
        out_specs=[VMEM] * 3,
        compiler_params=PARAMS,
        cost_estimate=cost(2 * 16 * plane // 4, 12 * plane),
    )(even, field, noise)
    first = lax.ppermute(inner, ("rep", "slab"), side_swap(0, size))
    second = lax.ppermute(outer, ("rep", "slab"), side_swap(1, size))
    result = jax.ShapeDtypeStruct((planes, height, width), jnp.float32)
    scratch = [pltpu.VMEM((2, height, width), jnp.float32), pltpu.SemaphoreType.DMA((2,))]
    rest, out = pl.pallas_call(
        near_kernel,
        out_shape=[pair, result],
        in_specs=[SMEM] + [VMEM] * 4,
        out_specs=[VMEM, HBM],
        scratch_shapes=[pltpu.VMEM((3, height, width), jnp.float32)] + scratch,
        compiler_params=PARAMS,
        cost_estimate=cost(5 * 16 * plane // 4, 20 * plane),
    )(even, field, edge, first, noise)
    kicks = jnp.concatenate([noise[1, :1], noise[1, 3:]])
    out = pl.pallas_call(
        far_kernel,
        out_shape=result,
        in_specs=[SMEM] + [VMEM] * 5 + [HBM],
        out_specs=HBM,
        scratch_shapes=[pltpu.VMEM((1, height, width), jnp.float32)] + scratch,
        input_output_aliases={6: 0},
        compiler_params=PARAMS,
        cost_estimate=cost(16 * plane // 4, 10 * plane),
    )(even, field, edge, second, kicks, rest, out)
    return out[None]


def solution(mesh):
    return jax.shard_map(
        shards,
        mesh=mesh,
        in_specs=(P("rep", "slab", None, None), P(), P(None, "rep", "slab", None, None)),
        out_specs=P("rep", "slab", None, None),
        check_vma=False,
    )
```

```python
import functools

import jax
import jax.numpy as jnp
from jax import lax
from jax.experimental import pallas as pl
from jax.experimental.pallas import tpu as pltpu
from jax.sharding import PartitionSpec as P

STEP_SIZE = 0.05
MASS_TERM = -0.5
COUPLING = 0.5
KICK = (2.0 * STEP_SIZE) ** 0.5
HALF = 16
STRIP = 128
VMEM = pl.BlockSpec(memory_space=pltpu.VMEM)
SMEM = pl.BlockSpec(memory_space=pltpu.SMEM)
HBM = pl.BlockSpec(memory_space=pl.ANY)
PARAMS = pltpu.CompilerParams(vmem_limit_bytes=10 * 1024 * 1024)


def cost(flops, size):
    return pl.CostEstimate(flops=flops, bytes_accessed=size, transcendentals=0)


def ring_order():
    return [((3 * y) % 8) * 2 + core for y in range(8) for core in range(2)]


def exchange(parts, order):
    groups = [[half * HALF + i for i in order] for half in range(2)]
    return lax.all_to_all(parts, "rep", split_axis=0, concat_axis=0, tiled=True, axis_index_groups=groups)


def resample_map(copy_counts):
    ids = jnp.arange(copy_counts.shape[0], dtype=jnp.int32)
    upto = ids[None, :] <= ids[:, None]
    extra = jnp.maximum(copy_counts - 1, 0)
    inclusive = jnp.sum(jnp.where(upto, extra[None, :], 0), axis=1)
    empty = (copy_counts == 0).astype(jnp.int32)
    rank = jnp.sum(jnp.where(upto, empty[None, :], 0), axis=1) - empty
    filled = jnp.sum((inclusive[None, :] <= rank[:, None]).astype(jnp.int32), axis=1)
    return jnp.where(copy_counts >= 1, ids, filled)


def routes(copy_counts, order):
    ids = jnp.arange(2 * HALF, dtype=jnp.int32)
    half = lax.axis_index("rep") // HALF
    place = jnp.array([order.index(i) for i in range(HALF)] * 2, jnp.int32)
    source_map = resample_map(copy_counts)
    crosses = source_map // HALF != ids // HALF
    asked = source_map[:, None] == ids[None, :]
    wanted = jnp.any(crosses[:, None] & asked, axis=0)
    count = jnp.sum(wanted.astype(jnp.int32))
    earlier = (ids[None, :] < ids[:, None]) & wanted[None, :]
    rank = jnp.sum(earlier.astype(jnp.int32), axis=1)
    mine = wanted & (ids // HALF == half)
    send = jnp.sum(jnp.where(mine[None, :] & (rank[None, :] == ids[:HALF, None]), place[None, :], 0), axis=1)
    target = jnp.array(order, jnp.int32) + half * HALF
    where_from = jnp.where(ids // HALF == half, place, HALF + rank)
    source = jnp.sum(jnp.where(target[:, None] == ids[None, :], source_map[None, :], 0), axis=1)
    pick = jnp.sum(jnp.where(source[:, None] == ids[None, :], where_from[None, :], 0), axis=1)
    return pick, send, count, jnp.any(wanted[:HALF])


def chosen_parts(spread, pick, send, count, upward):
    def kept(spread, pick, send):
        return jnp.take(spread, pick, axis=0, mode="clip")

    def crossing(width, source, spread, pick, send):
        pairs = [(source * HALF + i, (1 - source) * HALF + i) for i in range(HALF)]
        far = lax.ppermute(jnp.take(spread, send[:width], axis=0, mode="clip"), "rep", pairs)
        if width == HALF:
            return jnp.take(jnp.concatenate([spread, far]), pick, axis=0, mode="clip")
        parts = kept(spread, pick, send)
        for i in range(width):
            parts = jnp.where((pick == HALF + i)[:, None, None], far[i : i + 1], parts)
        return parts

    widths = (1, 2, 3, 4, 6, HALF)
    case = sum((count > w).astype(jnp.int32) for w in widths[:-1])
    case = jnp.where(count == 0, 0, 1 + case + jnp.where(upward, 0, len(widths)))
    branches = [kept] + [functools.partial(crossing, w, source) for source in range(2) for w in widths]
    return lax.switch(case, branches, spread, pick, send)


def step(ref, plane, start, along_z, kicks):
    rows = lambda first, size: ref[plane, pl.ds(pl.multiple_of(first, 8), size), :]
    center = rows(start, STRIP)
    block = jnp.concatenate([rows((start + 248) % 256, 8), center, rows((start + STRIP) % 256, 8)])
    above = pltpu.roll(block, STRIP + 15, 0)[8 : 8 + STRIP]
    below = pltpu.roll(block, 1, 0)[8 : 8 + STRIP]
    right, left = pltpu.roll(center, 255, 1), pltpu.roll(center, 1, 1)
    laplace = along_z + above + below + right + left - 6.0 * center
    drift = laplace - MASS_TERM * center - COUPLING * center * center * center
    return center + STEP_SIZE * drift + kicks


def strips(body):
    @pl.loop(0, 256 // STRIP)
    def _(i):
        start = pl.multiple_of(i * STRIP, STRIP)
        body(start, pl.ds(start, STRIP))


def edge_kernel(even, field, noise, edge, inner, outer):
    def fill(below, above):
        def body(start, here):
            low = step(field, 0, start, field[1, here, :], KICK * noise[0, 0, here, :])
            high = step(field, 3, start, field[2, here, :], KICK * noise[0, 3, here, :])
            edge[0, here, :] = low
            edge[1, here, :] = high
            below[0, here, :] = field[0, here, :]
            below[1, here, :] = low
            above[0, here, :] = field[3, here, :]
            above[1, here, :] = high

        strips(body)

    @pl.when(even[0] == 1)
    def _():
        fill(outer, inner)

    @pl.when(even[0] == 0)
    def _():
        fill(inner, outer)


def near_kernel(even, field, edge, first, noise, rest, out, middle, ends, sems):
    def inside(start, here):
        for plane in (1, 2):
            along_z = field[plane + 1, here, :] + field[plane - 1, here, :]
            middle[plane - 1, here, :] = step(field, plane, start, along_z, KICK * noise[0, plane, here, :])

    def side(end, near, far):
        def completed(start, here):
            swept_end = edge[end // 3, here, :] + STEP_SIZE * first[0, here, :]
            middle[2, here, :] = swept_end
            inner = step(middle, near - 1, start, middle[far - 1, here, :], KICK * noise[1, near, here, :])
            ends[1, here, :] = inner + STEP_SIZE * swept_end
            rest[0, here, :] = middle[far - 1, here, :]
            rest[1, here, :] = step(middle, far - 1, start, middle[near - 1, here, :], KICK * noise[1, far, here, :])

        def last(start, here):
            beyond = first[1, here, :] + STEP_SIZE * field[end, here, :]
            along_z = middle[near - 1, here, :] + beyond
            ends[0, here, :] = step(middle, 2, start, along_z, KICK * noise[1, end, here, :])

        strips(completed)
        inner_copy = pltpu.make_async_copy(ends.at[1], out.at[near], sems.at[1])
        inner_copy.start()
        strips(last)
        end_copy = pltpu.make_async_copy(ends.at[0], out.at[end], sems.at[0])
        end_copy.start()
        inner_copy.wait()
        end_copy.wait()

    strips(inside)

    @pl.when(even[0] == 1)
    def _():
        side(3, 2, 1)

    @pl.when(even[0] == 0)
    def _():
        side(0, 1, 2)


def far_kernel(even, field, edge, second, kicks, rest, started, out, whole, ends, sems):
    def side(end, inner):
        def completed(start, here):
            swept_end = edge[end // 3, here, :] + STEP_SIZE * second[0, here, :]
            whole[0, here, :] = swept_end
            ends[1, here, :] = rest[1, here, :] + STEP_SIZE * swept_end

        def last(start, here):
            beyond = second[1, here, :] + STEP_SIZE * field[end, here, :]
            ends[0, here, :] = step(whole, 0, start, rest[0, here, :] + beyond, KICK * kicks[end // 3, here, :])

        strips(completed)
        inner_copy = pltpu.make_async_copy(ends.at[1], out.at[inner], sems.at[1])
        inner_copy.start()
        strips(last)
        end_copy = pltpu.make_async_copy(ends.at[0], out.at[end], sems.at[0])
        end_copy.start()
        inner_copy.wait()
        end_copy.wait()

    @pl.when(even[0] == 1)
    def _():
        side(0, 1)

    @pl.when(even[0] == 0)
    def _():
        side(3, 2)


def side_swap(turn, size):
    pairs = []
    for rep in range(2 * HALF):
        for slab in range(size):
            above = (slab + rep + turn) % 2 == 0
            pairs.append((rep * size + slab, rep * size + (slab + (1 if above else -1)) % size))
    return pairs


def shards(phi_field, copy_counts, langevin_noise):
    planes, height, width = phi_field.shape[1:]
    size = lax.axis_size("slab")
    order = ring_order()
    noise = langevin_noise[:, 0]
    spread = exchange(phi_field.reshape(HALF, -1, width), order)
    route = routes(copy_counts, order)
    field = exchange(chosen_parts(spread, *route), order).reshape(planes, height, width)
    even = ((lax.axis_index("slab") + lax.axis_index("rep")) % 2 == 0).astype(jnp.int32).reshape(1)
    pair = jax.ShapeDtypeStruct((2, height, width), jnp.float32)
    plane = 4 * height * width
    edge, inner, outer = pl.pallas_call(
        edge_kernel,
        out_shape=[pair] * 3,
        in_specs=[SMEM] + [VMEM] * 2,
        out_specs=[VMEM] * 3,
        compiler_params=PARAMS,
        cost_estimate=cost(2 * 16 * plane // 4, 12 * plane),
    )(even, field, noise)
    first = lax.ppermute(inner, ("rep", "slab"), side_swap(0, size))
    second = lax.ppermute(outer, ("rep", "slab"), side_swap(1, size))
    result = jax.ShapeDtypeStruct((planes, height, width), jnp.float32)
    scratch = [pltpu.VMEM((2, height, width), jnp.float32), pltpu.SemaphoreType.DMA((2,))]
    rest, out = pl.pallas_call(
        near_kernel,
        out_shape=[pair, result],
        in_specs=[SMEM] + [VMEM] * 4,
        out_specs=[VMEM, HBM],
        scratch_shapes=[pltpu.VMEM((3, height, width), jnp.float32)] + scratch,
        compiler_params=PARAMS,
        cost_estimate=cost(5 * 16 * plane // 4, 20 * plane),
    )(even, field, edge, first, noise)
    kicks = jnp.concatenate([noise[1, :1], noise[1, 3:]])
    out = pl.pallas_call(
        far_kernel,
        out_shape=result,
        in_specs=[SMEM] + [VMEM] * 5 + [HBM],
        out_specs=HBM,
        scratch_shapes=[pltpu.VMEM((1, height, width), jnp.float32)] + scratch,
        input_output_aliases={6: 0},
        compiler_params=PARAMS,
        cost_estimate=cost(16 * plane // 4, 10 * plane),
    )(even, field, edge, second, kicks, rest, out)
    return out[None]


def solution(mesh):
    return jax.shard_map(
        shards,
        mesh=mesh,
        in_specs=(P("rep", "slab", None, None), P(), P(None, "rep", "slab", None, None)),
        out_specs=P("rep", "slab", None, None),
        check_vma=False,
    )
```

```python
import functools

import jax
import jax.numpy as jnp
from jax import lax
from jax.experimental import pallas as pl
from jax.experimental.pallas import tpu as pltpu
from jax.sharding import PartitionSpec as P

STEP_SIZE = 0.05
MASS_TERM = -0.5
COUPLING = 0.5
KICK = (2.0 * STEP_SIZE) ** 0.5
HALF = 16
STRIP = 128
VMEM = pl.BlockSpec(memory_space=pltpu.VMEM)
SMEM = pl.BlockSpec(memory_space=pltpu.SMEM)
HBM = pl.BlockSpec(memory_space=pl.ANY)
PARAMS = pltpu.CompilerParams(vmem_limit_bytes=10 * 1024 * 1024)


def cost(flops, size):
    return pl.CostEstimate(flops=flops, bytes_accessed=size, transcendentals=0)


def ring_order():
    return [((3 * y) % 8) * 2 + core for y in range(8) for core in range(2)]


def exchange(parts, order):
    groups = [[half * HALF + i for i in order] for half in range(2)]
    return lax.all_to_all(parts, "rep", split_axis=0, concat_axis=0, tiled=True, axis_index_groups=groups)


def resample_map(copy_counts):
    ids = jnp.arange(copy_counts.shape[0], dtype=jnp.int32)
    upto = ids[None, :] <= ids[:, None]
    extra = jnp.maximum(copy_counts - 1, 0)
    inclusive = jnp.sum(jnp.where(upto, extra[None, :], 0), axis=1)
    empty = (copy_counts == 0).astype(jnp.int32)
    rank = jnp.sum(jnp.where(upto, empty[None, :], 0), axis=1) - empty
    filled = jnp.sum((inclusive[None, :] <= rank[:, None]).astype(jnp.int32), axis=1)
    return jnp.where(copy_counts >= 1, ids, filled)


def routes(copy_counts, order):
    ids = jnp.arange(2 * HALF, dtype=jnp.int32)
    half = lax.axis_index("rep") // HALF
    place = jnp.array([order.index(i) for i in range(HALF)] * 2, jnp.int32)
    source_map = resample_map(copy_counts)
    crosses = source_map // HALF != ids // HALF
    asked = source_map[:, None] == ids[None, :]
    wanted = jnp.any(crosses[:, None] & asked, axis=0)
    count = jnp.sum(wanted.astype(jnp.int32))
    earlier = (ids[None, :] < ids[:, None]) & wanted[None, :]
    rank = jnp.sum(earlier.astype(jnp.int32), axis=1)
    mine = wanted & (ids // HALF == half)
    send = jnp.sum(jnp.where(mine[None, :] & (rank[None, :] == ids[:HALF, None]), place[None, :], 0), axis=1)
    target = jnp.array(order, jnp.int32) + half * HALF
    where_from = jnp.where(ids // HALF == half, place, HALF + rank)
    source = jnp.sum(jnp.where(target[:, None] == ids[None, :], source_map[None, :], 0), axis=1)
    pick = jnp.sum(jnp.where(source[:, None] == ids[None, :], where_from[None, :], 0), axis=1)
    return pick, send, count, jnp.any(wanted[:HALF])


def chosen_parts(spread, pick, send, count, upward):
    def kept(spread, pick, send):
        return jnp.take(spread, pick, axis=0, mode="clip")

    def crossing(width, source, spread, pick, send):
        pairs = [(source * HALF + i, (1 - source) * HALF + i) for i in range(HALF)]
        far = lax.ppermute(jnp.take(spread, send[:width], axis=0, mode="clip"), "rep", pairs)
        if width == HALF:
            return jnp.take(jnp.concatenate([spread, far]), pick, axis=0, mode="clip")
        parts = kept(spread, pick, send)
        for i in range(width):
            parts = jnp.where((pick == HALF + i)[:, None, None], far[i : i + 1], parts)
        return parts

    widths = (1, 2, 3, 4, 6, HALF)
    case = sum((count > w).astype(jnp.int32) for w in widths[:-1])
    case = jnp.where(count == 0, 0, 1 + case + jnp.where(upward, 0, len(widths)))
    branches = [kept] + [functools.partial(crossing, w, source) for source in range(2) for w in widths]
    return lax.switch(case, branches, spread, pick, send)


def step(ref, plane, start, along_z, kicks):
    rows = lambda first, size: ref[plane, pl.ds(pl.multiple_of(first, 8), size), :]
    center = rows(start, STRIP)
    block = jnp.concatenate([rows((start + 248) % 256, 8), center, rows((start + STRIP) % 256, 8)])
    above = pltpu.roll(block, STRIP + 15, 0)[8 : 8 + STRIP]
    below = pltpu.roll(block, 1, 0)[8 : 8 + STRIP]
    right, left = pltpu.roll(center, 255, 1), pltpu.roll(center, 1, 1)
    laplace = along_z + above + below + right + left - 6.0 * center
    drift = laplace - MASS_TERM * center - COUPLING * center * center * center
    return center + STEP_SIZE * drift + kicks


def strips(body):
    @pl.loop(0, 256 // STRIP)
    def _(i):
        start = pl.multiple_of(i * STRIP, STRIP)
        body(start, pl.ds(start, STRIP))


def edge_kernel(above, field, noise, *refs):
    sent = refs[-1]

    def fill(plane, inward):
        def body(start, here):
            sent[0, here, :] = field[plane, here, :]
            sent[1, here, :] = step(field, plane, start, field[inward, here, :], KICK * noise[0, plane, here, :])

        strips(body)

    @pl.when(above[0] == 1)
    def _():
        fill(3, 2)

    @pl.when(above[0] == 0)
    def _():
        fill(0, 1)


def near_kernel(even, field, sent, first, noise, rest, out, middle, ends, sems):
    def inside(start, here):
        for plane in (1, 2):
            along_z = field[plane + 1, here, :] + field[plane - 1, here, :]
            middle[plane - 1, here, :] = step(field, plane, start, along_z, KICK * noise[0, plane, here, :])

    def side(end, near, far):
        def completed(start, here):
            swept_end = sent[1, here, :] + STEP_SIZE * first[0, here, :]
            middle[2, here, :] = swept_end
            inner = step(middle, near - 1, start, middle[far - 1, here, :], KICK * noise[1, near, here, :])
            ends[1, here, :] = inner + STEP_SIZE * swept_end
            rest[0, here, :] = middle[far - 1, here, :]
            rest[1, here, :] = step(middle, far - 1, start, middle[near - 1, here, :], KICK * noise[1, far, here, :])

        def last(start, here):
            beyond = first[1, here, :] + STEP_SIZE * sent[0, here, :]
            along_z = middle[near - 1, here, :] + beyond
            ends[0, here, :] = step(middle, 2, start, along_z, KICK * noise[1, end, here, :])

        strips(completed)
        inner_copy = pltpu.make_async_copy(ends.at[1], out.at[near], sems.at[1])
        inner_copy.start()
        strips(last)
        end_copy = pltpu.make_async_copy(ends.at[0], out.at[end], sems.at[0])
        end_copy.start()
        inner_copy.wait()
        end_copy.wait()

    strips(inside)

    @pl.when(even[0] == 1)
    def _():
        side(3, 2, 1)

    @pl.when(even[0] == 0)
    def _():
        side(0, 1, 2)


def far_kernel(even, sent, second, kicks, rest, started, out, whole, ends, sems):
    def side(end, inner):
        def completed(start, here):
            swept_end = sent[1, here, :] + STEP_SIZE * second[0, here, :]
            whole[0, here, :] = swept_end
            ends[1, here, :] = rest[1, here, :] + STEP_SIZE * swept_end

        def last(start, here):
            beyond = second[1, here, :] + STEP_SIZE * sent[0, here, :]
            ends[0, here, :] = step(whole, 0, start, rest[0, here, :] + beyond, KICK * kicks[end // 3, here, :])

        strips(completed)
        inner_copy = pltpu.make_async_copy(ends.at[1], out.at[inner], sems.at[1])
        inner_copy.start()
        strips(last)
        end_copy = pltpu.make_async_copy(ends.at[0], out.at[end], sems.at[0])
        end_copy.start()
        inner_copy.wait()
        end_copy.wait()

    @pl.when(even[0] == 1)
    def _():
        side(0, 1)

    @pl.when(even[0] == 0)
    def _():
        side(3, 2)


def side_swap(turn, size):
    pairs = []
    for rep in range(2 * HALF):
        for slab in range(size):
            above = (slab + rep + turn) % 2 == 0
            pairs.append((rep * size + slab, rep * size + (slab + (1 if above else -1)) % size))
    return pairs


def shards(phi_field, copy_counts, langevin_noise):
    planes, height, width = phi_field.shape[1:]
    size = lax.axis_size("slab")
    order = ring_order()
    noise = langevin_noise[:, 0]
    spread = exchange(phi_field.reshape(HALF, -1, width), order)
    route = routes(copy_counts, order)
    field = exchange(chosen_parts(spread, *route), order).reshape(planes, height, width)
    even = ((lax.axis_index("slab") + lax.axis_index("rep")) % 2 == 0).astype(jnp.int32).reshape(1)
    pair = jax.ShapeDtypeStruct((2, height, width), jnp.float32)
    plane = 4 * height * width
    def made(above, *after):
        return pl.pallas_call(
            edge_kernel,
            out_shape=pair,
            in_specs=[SMEM] + [VMEM] * 2 + [HBM] * len(after),
            out_specs=VMEM,
            compiler_params=PARAMS,
            cost_estimate=cost(16 * plane // 4, 5 * plane),
        )(above, field, noise, *after)

    inner = made(even)
    outer = made(1 - even, inner)
    first = lax.ppermute(inner, ("rep", "slab"), side_swap(0, size))
    second = lax.ppermute(outer, ("rep", "slab"), side_swap(1, size))
    result = jax.ShapeDtypeStruct((planes, height, width), jnp.float32)
    scratch = [pltpu.VMEM((2, height, width), jnp.float32), pltpu.SemaphoreType.DMA((2,))]
    rest, out = pl.pallas_call(
        near_kernel,
        out_shape=[pair, result],
        in_specs=[SMEM] + [VMEM] * 4,
        out_specs=[VMEM, HBM],
        scratch_shapes=[pltpu.VMEM((3, height, width), jnp.float32)] + scratch,
        compiler_params=PARAMS,
        cost_estimate=cost(5 * 16 * plane // 4, 20 * plane),
    )(even, field, inner, first, noise)
    kicks = jnp.concatenate([noise[1, :1], noise[1, 3:]])
    out = pl.pallas_call(
        far_kernel,
        out_shape=result,
        in_specs=[SMEM] + [VMEM] * 4 + [HBM],
        out_specs=HBM,
        scratch_shapes=[pltpu.VMEM((1, height, width), jnp.float32)] + scratch,
        input_output_aliases={5: 0},
        compiler_params=PARAMS,
        cost_estimate=cost(16 * plane // 4, 10 * plane),
    )(even, outer, second, kicks, rest, out)
    return out[None]


def solution(mesh):
    return jax.shard_map(
        shards,
        mesh=mesh,
        in_specs=(P("rep", "slab", None, None), P(), P(None, "rep", "slab", None, None)),
        out_specs=P("rep", "slab", None, None),
        check_vma=False,
    )
```

```python
import functools

import jax
import jax.numpy as jnp
from jax import lax
from jax.experimental import pallas as pl
from jax.experimental.pallas import tpu as pltpu
from jax.sharding import PartitionSpec as P

STEP_SIZE = 0.05
MASS_TERM = -0.5
COUPLING = 0.5
KICK = (2.0 * STEP_SIZE) ** 0.5
HALF = 16
STRIP = 256
VMEM = pl.BlockSpec(memory_space=pltpu.VMEM)
SMEM = pl.BlockSpec(memory_space=pltpu.SMEM)
HBM = pl.BlockSpec(memory_space=pl.ANY)
PARAMS = pltpu.CompilerParams(vmem_limit_bytes=10 * 1024 * 1024)


def cost(flops, size):
    return pl.CostEstimate(flops=flops, bytes_accessed=size, transcendentals=0)


def ring_order():
    return [((3 * y) % 8) * 2 + core for y in range(8) for core in range(2)]


def exchange(parts, order):
    groups = [[half * HALF + i for i in order] for half in range(2)]
    return lax.all_to_all(parts, "rep", split_axis=0, concat_axis=0, tiled=True, axis_index_groups=groups)


def resample_map(copy_counts):
    ids = jnp.arange(copy_counts.shape[0], dtype=jnp.int32)
    upto = ids[None, :] <= ids[:, None]
    extra = jnp.maximum(copy_counts - 1, 0)
    inclusive = jnp.sum(jnp.where(upto, extra[None, :], 0), axis=1)
    empty = (copy_counts == 0).astype(jnp.int32)
    rank = jnp.sum(jnp.where(upto, empty[None, :], 0), axis=1) - empty
    filled = jnp.sum((inclusive[None, :] <= rank[:, None]).astype(jnp.int32), axis=1)
    return jnp.where(copy_counts >= 1, ids, filled)


def routes(copy_counts, order):
    ids = jnp.arange(2 * HALF, dtype=jnp.int32)
    half = lax.axis_index("rep") // HALF
    place = jnp.array([order.index(i) for i in range(HALF)] * 2, jnp.int32)
    source_map = resample_map(copy_counts)
    crosses = source_map // HALF != ids // HALF
    asked = source_map[:, None] == ids[None, :]
    wanted = jnp.any(crosses[:, None] & asked, axis=0)
    count = jnp.sum(wanted.astype(jnp.int32))
    earlier = (ids[None, :] < ids[:, None]) & wanted[None, :]
    rank = jnp.sum(earlier.astype(jnp.int32), axis=1)
    mine = wanted & (ids // HALF == half)
    send = jnp.sum(jnp.where(mine[None, :] & (rank[None, :] == ids[:HALF, None]), place[None, :], 0), axis=1)
    target = jnp.array(order, jnp.int32) + half * HALF
    where_from = jnp.where(ids // HALF == half, place, HALF + rank)
    source = jnp.sum(jnp.where(target[:, None] == ids[None, :], source_map[None, :], 0), axis=1)
    pick = jnp.sum(jnp.where(source[:, None] == ids[None, :], where_from[None, :], 0), axis=1)
    return pick, send, count, jnp.any(wanted[:HALF])


def chosen_parts(spread, pick, send, count, upward):
    def kept(spread, pick, send):
        return jnp.take(spread, pick, axis=0, mode="clip")

    def crossing(width, source, spread, pick, send):
        pairs = [(source * HALF + i, (1 - source) * HALF + i) for i in range(HALF)]
        far = lax.ppermute(jnp.take(spread, send[:width], axis=0, mode="clip"), "rep", pairs)
        if width == HALF:
            return jnp.take(jnp.concatenate([spread, far]), pick, axis=0, mode="clip")
        parts = kept(spread, pick, send)
        for i in range(width):
            parts = jnp.where((pick == HALF + i)[:, None, None], far[i : i + 1], parts)
        return parts

    widths = (1, 2, 3, 4, 6, HALF)
    case = sum((count > w).astype(jnp.int32) for w in widths[:-1])
    case = jnp.where(count == 0, 0, 1 + case + jnp.where(upward, 0, len(widths)))
    branches = [kept] + [functools.partial(crossing, w, source) for source in range(2) for w in widths]
    return lax.switch(case, branches, spread, pick, send)


def step(ref, plane, start, along_z, kicks):
    rows = lambda first, size: ref[plane, pl.ds(pl.multiple_of(first, 8), size), :]
    center = rows(start, STRIP)
    block = jnp.concatenate([rows((start + 248) % 256, 8), center, rows((start + STRIP) % 256, 8)])
    above = pltpu.roll(block, STRIP + 15, 0)[8 : 8 + STRIP]
    below = pltpu.roll(block, 1, 0)[8 : 8 + STRIP]
    right, left = pltpu.roll(center, 255, 1), pltpu.roll(center, 1, 1)
    laplace = along_z + above + below + right + left - 6.0 * center
    drift = laplace - MASS_TERM * center - COUPLING * center * center * center
    return center + STEP_SIZE * drift + kicks


def strips(body):
    @pl.loop(0, 256 // STRIP)
    def _(i):
        start = pl.multiple_of(i * STRIP, STRIP)
        body(start, pl.ds(start, STRIP))


def edge_kernel(above, field, noise, *refs):
    sent = refs[-1]

    def fill(plane, inward):
        def body(start, here):
            sent[0, here, :] = field[plane, here, :]
            sent[1, here, :] = step(field, plane, start, field[inward, here, :], KICK * noise[0, plane, here, :])

        strips(body)

    @pl.when(above[0] == 1)
    def _():
        fill(3, 2)

    @pl.when(above[0] == 0)
    def _():
        fill(0, 1)


def near_kernel(even, field, sent, first, noise, rest, out, middle, ends, sems):
    def inside(start, here):
        for plane in (1, 2):
            along_z = field[plane + 1, here, :] + field[plane - 1, here, :]
            middle[plane - 1, here, :] = step(field, plane, start, along_z, KICK * noise[0, plane, here, :])

    def side(end, near, far):
        def completed(start, here):
            swept_end = sent[1, here, :] + STEP_SIZE * first[0, here, :]
            middle[2, here, :] = swept_end
            inner = step(middle, near - 1, start, middle[far - 1, here, :], KICK * noise[1, near, here, :])
            ends[1, here, :] = inner + STEP_SIZE * swept_end
            rest[0, here, :] = middle[far - 1, here, :]
            rest[1, here, :] = step(middle, far - 1, start, middle[near - 1, here, :], KICK * noise[1, far, here, :])

        def last(start, here):
            beyond = first[1, here, :] + STEP_SIZE * sent[0, here, :]
            along_z = middle[near - 1, here, :] + beyond
            ends[0, here, :] = step(middle, 2, start, along_z, KICK * noise[1, end, here, :])

        strips(completed)
        inner_copy = pltpu.make_async_copy(ends.at[1], out.at[near], sems.at[1])
        inner_copy.start()
        strips(last)
        end_copy = pltpu.make_async_copy(ends.at[0], out.at[end], sems.at[0])
        end_copy.start()
        inner_copy.wait()
        end_copy.wait()

    strips(inside)

    @pl.when(even[0] == 1)
    def _():
        side(3, 2, 1)

    @pl.when(even[0] == 0)
    def _():
        side(0, 1, 2)


def far_kernel(even, sent, second, kicks, rest, started, out, whole, ends, sems):
    def side(end, inner):
        def completed(start, here):
            swept_end = sent[1, here, :] + STEP_SIZE * second[0, here, :]
            whole[0, here, :] = swept_end
            ends[1, here, :] = rest[1, here, :] + STEP_SIZE * swept_end

        def last(start, here):
            beyond = second[1, here, :] + STEP_SIZE * sent[0, here, :]
            ends[0, here, :] = step(whole, 0, start, rest[0, here, :] + beyond, KICK * kicks[end // 3, here, :])

        strips(completed)
        inner_copy = pltpu.make_async_copy(ends.at[1], out.at[inner], sems.at[1])
        inner_copy.start()
        strips(last)
        end_copy = pltpu.make_async_copy(ends.at[0], out.at[end], sems.at[0])
        end_copy.start()
        inner_copy.wait()
        end_copy.wait()

    @pl.when(even[0] == 1)
    def _():
        side(0, 1)

    @pl.when(even[0] == 0)
    def _():
        side(3, 2)


def side_swap(turn, size):
    pairs = []
    for rep in range(2 * HALF):
        for slab in range(size):
            above = (slab + rep + turn) % 2 == 0
            pairs.append((rep * size + slab, rep * size + (slab + (1 if above else -1)) % size))
    return pairs


def shards(phi_field, copy_counts, langevin_noise):
    planes, height, width = phi_field.shape[1:]
    size = lax.axis_size("slab")
    order = ring_order()
    noise = langevin_noise[:, 0]
    spread = exchange(phi_field.reshape(HALF, -1, width), order)
    route = routes(copy_counts, order)
    field = exchange(chosen_parts(spread, *route), order).reshape(planes, height, width)
    even = ((lax.axis_index("slab") + lax.axis_index("rep")) % 2 == 0).astype(jnp.int32).reshape(1)
    pair = jax.ShapeDtypeStruct((2, height, width), jnp.float32)
    plane = 4 * height * width
    def made(above, *after):
        return pl.pallas_call(
            edge_kernel,
            out_shape=pair,
            in_specs=[SMEM] + [VMEM] * 2 + [HBM] * len(after),
            out_specs=VMEM,
            compiler_params=PARAMS,
            cost_estimate=cost(16 * plane // 4, 5 * plane),
        )(above, field, noise, *after)

    inner = made(even)
    outer = made(1 - even, inner)
    first = lax.ppermute(inner, ("rep", "slab"), side_swap(0, size))
    second = lax.ppermute(outer, ("rep", "slab"), side_swap(1, size))
    result = jax.ShapeDtypeStruct((planes, height, width), jnp.float32)
    scratch = [pltpu.VMEM((2, height, width), jnp.float32), pltpu.SemaphoreType.DMA((2,))]
    rest, out = pl.pallas_call(
        near_kernel,
        out_shape=[pair, result],
        in_specs=[SMEM] + [VMEM] * 4,
        out_specs=[VMEM, HBM],
        scratch_shapes=[pltpu.VMEM((3, height, width), jnp.float32)] + scratch,
        compiler_params=PARAMS,
        cost_estimate=cost(5 * 16 * plane // 4, 20 * plane),
    )(even, field, inner, first, noise)
    kicks = jnp.concatenate([noise[1, :1], noise[1, 3:]])
    out = pl.pallas_call(
        far_kernel,
        out_shape=result,
        in_specs=[SMEM] + [VMEM] * 4 + [HBM],
        out_specs=HBM,
        scratch_shapes=[pltpu.VMEM((1, height, width), jnp.float32)] + scratch,
        input_output_aliases={5: 0},
        compiler_params=PARAMS,
        cost_estimate=cost(16 * plane // 4, 10 * plane),
    )(even, outer, second, kicks, rest, out)
    return out[None]


def solution(mesh):
    return jax.shard_map(
        shards,
        mesh=mesh,
        in_specs=(P("rep", "slab", None, None), P(), P(None, "rep", "slab", None, None)),
        out_specs=P("rep", "slab", None, None),
        check_vma=False,
    )
```

```python
import functools

import jax
import jax.numpy as jnp
from jax import lax
from jax.experimental import pallas as pl
from jax.experimental.pallas import tpu as pltpu
from jax.sharding import PartitionSpec as P

STEP_SIZE = 0.05
MASS_TERM = -0.5
COUPLING = 0.5
KICK = (2.0 * STEP_SIZE) ** 0.5
HALF = 16
STRIP = 128
VMEM = pl.BlockSpec(memory_space=pltpu.VMEM)
SMEM = pl.BlockSpec(memory_space=pltpu.SMEM)
HBM = pl.BlockSpec(memory_space=pl.ANY)
PARAMS = pltpu.CompilerParams(vmem_limit_bytes=10 * 1024 * 1024)


def cost(flops, size):
    return pl.CostEstimate(flops=flops, bytes_accessed=size, transcendentals=0)


def ring_order():
    return [(3 * y % 8) * 2 for y in range(8)] + [y * 2 + 1 for y in range(8)]


def exchange(parts, order):
    groups = [[half * HALF + i for i in order] for half in range(2)]
    return lax.all_to_all(parts, "rep", split_axis=0, concat_axis=0, tiled=True, axis_index_groups=groups)


def resample_map(copy_counts):
    ids = jnp.arange(copy_counts.shape[0], dtype=jnp.int32)
    upto = ids[None, :] <= ids[:, None]
    extra = jnp.maximum(copy_counts - 1, 0)
    inclusive = jnp.sum(jnp.where(upto, extra[None, :], 0), axis=1)
    empty = (copy_counts == 0).astype(jnp.int32)
    rank = jnp.sum(jnp.where(upto, empty[None, :], 0), axis=1) - empty
    filled = jnp.sum((inclusive[None, :] <= rank[:, None]).astype(jnp.int32), axis=1)
    return jnp.where(copy_counts >= 1, ids, filled)


def routes(copy_counts, order):
    ids = jnp.arange(2 * HALF, dtype=jnp.int32)
    half = lax.axis_index("rep") // HALF
    place = jnp.array([order.index(i) for i in range(HALF)] * 2, jnp.int32)
    source_map = resample_map(copy_counts)
    crosses = source_map // HALF != ids // HALF
    asked = source_map[:, None] == ids[None, :]
    wanted = jnp.any(crosses[:, None] & asked, axis=0)
    count = jnp.sum(wanted.astype(jnp.int32))
    earlier = (ids[None, :] < ids[:, None]) & wanted[None, :]
    rank = jnp.sum(earlier.astype(jnp.int32), axis=1)
    mine = wanted & (ids // HALF == half)
    send = jnp.sum(jnp.where(mine[None, :] & (rank[None, :] == ids[:HALF, None]), place[None, :], 0), axis=1)
    target = jnp.array(order, jnp.int32) + half * HALF
    where_from = jnp.where(ids // HALF == half, place, HALF + rank)
    source = jnp.sum(jnp.where(target[:, None] == ids[None, :], source_map[None, :], 0), axis=1)
    pick = jnp.sum(jnp.where(source[:, None] == ids[None, :], where_from[None, :], 0), axis=1)
    return pick, send, count, jnp.any(wanted[:HALF])


def chosen_parts(spread, pick, send, count, upward):
    def kept(spread, pick, send):
        return jnp.take(spread, pick, axis=0, mode="clip")

    def crossing(width, source, spread, pick, send):
        pairs = [(source * HALF + i, (1 - source) * HALF + i) for i in range(HALF)]
        far = lax.ppermute(jnp.take(spread, send[:width], axis=0, mode="clip"), "rep", pairs)
        if width == HALF:
            return jnp.take(jnp.concatenate([spread, far]), pick, axis=0, mode="clip")
        parts = kept(spread, pick, send)
        for i in range(width):
            parts = jnp.where((pick == HALF + i)[:, None, None], far[i : i + 1], parts)
        return parts

    widths = (1, 2, 3, 4, 6, HALF)
    case = sum((count > w).astype(jnp.int32) for w in widths[:-1])
    case = jnp.where(count == 0, 0, 1 + case + jnp.where(upward, 0, len(widths)))
    branches = [kept] + [functools.partial(crossing, w, source) for source in range(2) for w in widths]
    return lax.switch(case, branches, spread, pick, send)


def step(ref, plane, start, along_z, kicks):
    rows = lambda first, size: ref[plane, pl.ds(pl.multiple_of(first, 8), size), :]
    center = rows(start, STRIP)
    block = jnp.concatenate([rows((start + 248) % 256, 8), center, rows((start + STRIP) % 256, 8)])
    above = pltpu.roll(block, STRIP + 15, 0)[8 : 8 + STRIP]
    below = pltpu.roll(block, 1, 0)[8 : 8 + STRIP]
    right, left = pltpu.roll(center, 255, 1), pltpu.roll(center, 1, 1)
    laplace = along_z + above + below + right + left - 6.0 * center
    drift = laplace - MASS_TERM * center - COUPLING * center * center * center
    return center + STEP_SIZE * drift + kicks


def strips(body):
    @pl.loop(0, 256 // STRIP)
    def _(i):
        start = pl.multiple_of(i * STRIP, STRIP)
        body(start, pl.ds(start, STRIP))


def edge_kernel(above, field, noise, *refs):
    sent = refs[-1]

    def fill(plane, inward):
        def body(start, here):
            sent[0, here, :] = field[plane, here, :]
            sent[1, here, :] = step(field, plane, start, field[inward, here, :], KICK * noise[0, plane, here, :])

        strips(body)

    @pl.when(above[0] == 1)
    def _():
        fill(3, 2)

    @pl.when(above[0] == 0)
    def _():
        fill(0, 1)


def near_kernel(even, field, sent, first, noise, rest, out, middle, ends, sems):
    def inside(start, here):
        for plane in (1, 2):
            along_z = field[plane + 1, here, :] + field[plane - 1, here, :]
            middle[plane - 1, here, :] = step(field, plane, start, along_z, KICK * noise[0, plane, here, :])

    def side(end, near, far):
        def completed(start, here):
            swept_end = sent[1, here, :] + STEP_SIZE * first[0, here, :]
            middle[2, here, :] = swept_end
            inner = step(middle, near - 1, start, middle[far - 1, here, :], KICK * noise[1, near, here, :])
            ends[1, here, :] = inner + STEP_SIZE * swept_end
            rest[0, here, :] = middle[far - 1, here, :]
            rest[1, here, :] = step(middle, far - 1, start, middle[near - 1, here, :], KICK * noise[1, far, here, :])

        def last(start, here):
            beyond = first[1, here, :] + STEP_SIZE * sent[0, here, :]
            along_z = middle[near - 1, here, :] + beyond
            ends[0, here, :] = step(middle, 2, start, along_z, KICK * noise[1, end, here, :])

        strips(completed)
        inner_copy = pltpu.make_async_copy(ends.at[1], out.at[near], sems.at[1])
        inner_copy.start()
        strips(last)
        end_copy = pltpu.make_async_copy(ends.at[0], out.at[end], sems.at[0])
        end_copy.start()
        inner_copy.wait()
        end_copy.wait()

    strips(inside)

    @pl.when(even[0] == 1)
    def _():
        side(3, 2, 1)

    @pl.when(even[0] == 0)
    def _():
        side(0, 1, 2)


def far_kernel(even, sent, second, kicks, rest, started, out, whole, ends, sems):
    def side(end, inner):
        def completed(start, here):
            swept_end = sent[1, here, :] + STEP_SIZE * second[0, here, :]
            whole[0, here, :] = swept_end
            ends[1, here, :] = rest[1, here, :] + STEP_SIZE * swept_end

        def last(start, here):
            beyond = second[1, here, :] + STEP_SIZE * sent[0, here, :]
            ends[0, here, :] = step(whole, 0, start, rest[0, here, :] + beyond, KICK * kicks[end // 3, here, :])

        strips(completed)
        inner_copy = pltpu.make_async_copy(ends.at[1], out.at[inner], sems.at[1])
        inner_copy.start()
        strips(last)
        end_copy = pltpu.make_async_copy(ends.at[0], out.at[end], sems.at[0])
        end_copy.start()
        inner_copy.wait()
        end_copy.wait()

    @pl.when(even[0] == 1)
    def _():
        side(0, 1)

    @pl.when(even[0] == 0)
    def _():
        side(3, 2)


def side_swap(turn, size):
    pairs = []
    for rep in range(2 * HALF):
        for slab in range(size):
            above = (slab + rep + turn) % 2 == 0
            pairs.append((rep * size + slab, rep * size + (slab + (1 if above else -1)) % size))
    return pairs


def shards(phi_field, copy_counts, langevin_noise):
    planes, height, width = phi_field.shape[1:]
    size = lax.axis_size("slab")
    order = ring_order()
    noise = langevin_noise[:, 0]
    spread = exchange(phi_field.reshape(HALF, -1, width), order)
    route = routes(copy_counts, order)
    field = exchange(chosen_parts(spread, *route), order).reshape(planes, height, width)
    even = ((lax.axis_index("slab") + lax.axis_index("rep")) % 2 == 0).astype(jnp.int32).reshape(1)
    pair = jax.ShapeDtypeStruct((2, height, width), jnp.float32)
    plane = 4 * height * width
    def made(above, *after):
        return pl.pallas_call(
            edge_kernel,
            out_shape=pair,
            in_specs=[SMEM] + [VMEM] * 2 + [HBM] * len(after),
            out_specs=VMEM,
            compiler_params=PARAMS,
            cost_estimate=cost(16 * plane // 4, 5 * plane),
        )(above, field, noise, *after)

    inner = made(even)
    outer = made(1 - even, inner)
    first = lax.ppermute(inner, ("rep", "slab"), side_swap(0, size))
    second = lax.ppermute(outer, ("rep", "slab"), side_swap(1, size))
    result = jax.ShapeDtypeStruct((planes, height, width), jnp.float32)
    scratch = [pltpu.VMEM((2, height, width), jnp.float32), pltpu.SemaphoreType.DMA((2,))]
    rest, out = pl.pallas_call(
        near_kernel,
        out_shape=[pair, result],
        in_specs=[SMEM] + [VMEM] * 4,
        out_specs=[VMEM, HBM],
        scratch_shapes=[pltpu.VMEM((3, height, width), jnp.float32)] + scratch,
        compiler_params=PARAMS,
        cost_estimate=cost(5 * 16 * plane // 4, 20 * plane),
    )(even, field, inner, first, noise)
    kicks = jnp.concatenate([noise[1, :1], noise[1, 3:]])
    out = pl.pallas_call(
        far_kernel,
        out_shape=result,
        in_specs=[SMEM] + [VMEM] * 4 + [HBM],
        out_specs=HBM,
        scratch_shapes=[pltpu.VMEM((1, height, width), jnp.float32)] + scratch,
        input_output_aliases={5: 0},
        compiler_params=PARAMS,
        cost_estimate=cost(16 * plane // 4, 10 * plane),
    )(even, outer, second, kicks, rest, out)
    return out[None]


def solution(mesh):
    return jax.shard_map(
        shards,
        mesh=mesh,
        in_specs=(P("rep", "slab", None, None), P(), P(None, "rep", "slab", None, None)),
        out_specs=P("rep", "slab", None, None),
        check_vma=False,
    )
```
